32 devices in a mesh: section: 2 (over x), dp: 4 (over z), tensor: 4 (over y, core).
Axes of the slice: x: 2, y: 2, z: 4, core: 2. Of those that a mesh axis runs over, the one named last changes fastest.
Arguments:
- vision_rows: bfloat16 [1024, 12800], P(('section', 'dp')), may hold values from -100 to 100
- vision_gain: float32 [12800], replicated, may hold values from 0.1 to 1.9
- vision_bias: float32 [12800], replicated, may hold values from -4 to 4
- proj_weight: bfloat16 [12800, 4096], P(('section', 'dp'), 'tensor'), may hold values from -0.0546875 to 0.0546875
- text_rows: bfloat16 [1024, 4096], P(('section', 'dp'), 'tensor'), may hold values from -100 to 100
- text_gain: float32 [4096], P('tensor'), may hold values from 0.1 to 1.9
- slot_of_row: int32 [1024], P(('section', 'dp')), may hold values from -1 to 1023, as said below
- out_cotangent: bfloat16 [1024, 4096], P(('section', 'dp'), 'tensor'), may hold values from -6 to 6
Outputs:
- normed: bfloat16 [1024, 4096], P(('section', 'dp'), 'tensor')
- vision_grad: bfloat16 [1024, 12800], P(('section', 'dp', 'tensor'))
The draws below stay inside these ranges and needn't reach their ends.
Inputs may be any that keep to these rules, and one draw needn't show every extreme that they name: `slot_of_row`: language device g (index g of section+dp) owns slots g * 128 to (g + 1) * 128 - 1. Rows come in aligned runs of 16: a run is all -1 or goes to 16 consecutive slots that start at a multiple of 16. A vision device sends only to language devices with the same dp index, at most 8 // 2 runs to each. No slot receives two rows. In every draw some vision device has all its runs live and some language device receives a row in every slot.
All inputs are finite; a program needn't handle non-finite values.
Results may differ from the reference program's by a relative error of at most 0.0064.
Values may be sent and summed in bfloat16 or wider, within the bound.
A program may use at most 128 MiB of HBM per device.

```python
import jax
import jax.numpy as jnp
from jax import lax

C = 12800
D = 4096
UNIT = 16
UNITS_DEV = 8
VROWS = 1024
LROWS = 1024
N_SECTION = 2
N_DP = 4


def rough_field(key, row_count, col_count, noise):
    first_key, second_key = jax.random.split(key, 2)
    row_scale = 10.0 ** (jax.random.uniform(first_key, (row_count, 1)) - 0.5)
    ramp = jnp.arange(col_count, dtype=jnp.float32) / max(col_count - 1, 1)
    col_scale = (3.0 ** ramp)[None, :] * 10.0 ** (jax.random.uniform(second_key, (1, col_count)) - 0.5)
    return jnp.clip(noise * row_scale * col_scale, -100.0, 100.0)


def draw_vision_rows(key, part):
    key = jax.random.fold_in(key, 3)
    noise_key, scale_key = jax.random.split(key, 2)
    noise = jax.random.normal(noise_key, (VROWS, C))
    return rough_field(scale_key, VROWS, C, noise).astype(jnp.bfloat16)


def draw_text_rows(key, part):
    key = jax.random.fold_in(key, 5)
    noise_key, scale_key = jax.random.split(key, 2)
    noise = jax.random.normal(noise_key, (LROWS, D))
    return rough_field(scale_key, LROWS, D, noise).astype(jnp.bfloat16)


def one_permutation(key, length):
    return jax.random.permutation(key, length)


def draw_slot_of_row(key, part):
    key = jax.random.fold_in(key, 7)
    keys = jax.random.split(key, 5)
    section_count = N_SECTION
    group_count = N_DP
    unit_count = UNITS_DEV
    orders = jax.vmap(one_permutation, in_axes=(0, None))(jax.random.split(keys[0], group_count), section_count)
    section_ids = jnp.arange(section_count)[:, None, None]
    group_ids = jnp.arange(group_count)[None, :, None]
    unit_ids = jnp.arange(unit_count)[None, None, :]
    offsets = jnp.transpose(orders)[:, :, None]
    target_section = (offsets + unit_ids) % section_count
    layouts = jax.vmap(one_permutation, in_axes=(0, None))(jax.random.split(keys[1], section_count * group_count), unit_count)
    lang_index = target_section * group_count + group_ids
    position = layouts[lang_index, jnp.broadcast_to(unit_ids, lang_index.shape)]
    coins = jax.random.randint(keys[2], (section_count, group_count, unit_count), 0, 100) < 55
    full_sender = jax.random.randint(keys[3], (1, group_count, 1), 0, section_count)
    full_receiver = jax.random.randint(keys[4], (1, group_count, 1), 0, section_count)
    live_units = coins | (section_ids == full_sender) | (target_section == full_receiver)
    run_start = lang_index * (unit_count * UNIT) + position * UNIT
    row_slots = run_start[..., None] + jnp.arange(UNIT)
    return jnp.where(live_units[..., None], row_slots, -1).reshape(-1).astype(jnp.int32)


def level_of(own_key, extent, cuts, least, high):
    level = 1.0
    for axis_at, parts in cuts:
        draws = jax.random.uniform(jax.random.fold_in(jax.random.fold_in(own_key, 6), axis_at), (parts,), jnp.float32, least / len(cuts), high / len(cuts))
        level = level * jnp.repeat(jnp.exp(draws), extent[axis_at] // parts).reshape((-1,) + (1,) * (len(extent) - 1 - axis_at))
    return level


def bell_draw(stream_key, extent, deviation, most, cuts=(), kind=jnp.bfloat16):
    entries = jax.random.normal(stream_key, extent, jnp.float32) * deviation
    if len(cuts) > 0:
        entries = level_of(stream_key, extent, cuts, -0.22, 0.18) * entries
    return jnp.clip(entries, min=-most, max=most).astype(kind)


def setup_inputs(seed: int = 0) -> dict:
    key_list = jax.random.split(jax.random.key(seed), 9)
    return {
        "vision_rows": draw_vision_rows(jax.random.fold_in(key_list[8], 71), 0),
        "vision_gain": jnp.clip(1.0 + 0.18 * jax.random.normal(key_list[1], (C,), jnp.float32), 0.1, 1.9),
        "vision_bias": bell_draw(key_list[2], (C,), 1.0, 4.0, (), jnp.float32),
        "proj_weight": bell_draw(key_list[3], (C, D), C ** -0.5, 0.0546875, ((0, 8), (1, 4))),
        "text_rows": draw_text_rows(jax.random.fold_in(key_list[8], 71), 0),
        "text_gain": jnp.clip(1.0 + 0.18 * jax.random.normal(key_list[5], (D,), jnp.float32), 0.1, 1.9),
        "slot_of_row": draw_slot_of_row(jax.random.fold_in(key_list[8], 71), 0),
        "out_cotangent": bell_draw(key_list[7], (LROWS, D), 1.0, 6.0, ((0, 8), (1, 4))),
    }


VISION_EPS = 1e-05
EPSILON = 1e-06
HALF_ROOT = 0.7071067811865476
INV_ROOT_TWO_PI = 0.3989422804014327

def gelu_value(values):
    return 0.5 * values * (1.0 + lax.erf(values * HALF_ROOT))

def gelu_slope(values):
    return 0.5 * (1.0 + lax.erf(values * HALF_ROOT)) + values * jnp.exp(-0.5 * values * values) * INV_ROOT_TWO_PI

def reference(vision_rows, vision_gain, vision_bias, proj_weight, text_rows, text_gain, slot_of_row, out_cotangent):
    vision_wide = vision_rows.astype(jnp.float32)
    centered = vision_wide - lax.optimization_barrier(jnp.mean(vision_wide, axis=1, keepdims=True))
    vision_inv = lax.rsqrt(lax.optimization_barrier(jnp.mean(centered * centered, axis=1, keepdims=True)) + VISION_EPS)
    vision_hat = centered * vision_inv
    normed_vision = (vision_hat * vision_gain + vision_bias).astype(jnp.bfloat16)
    projected = jnp.dot(normed_vision, proj_weight, preferred_element_type=jnp.float32)
    features = gelu_value(projected).astype(jnp.bfloat16)
    live_rows = slot_of_row >= 0
    target = jnp.where(live_rows, slot_of_row, LROWS).astype(jnp.int32)
    hidden = text_rows.at[target].set(features, mode='drop')
    hidden_wide = hidden.astype(jnp.float32)
    hidden_inv = lax.rsqrt(lax.optimization_barrier(jnp.mean(hidden_wide * hidden_wide, axis=1, keepdims=True)) + EPSILON)
    normed = (hidden_wide * hidden_inv * text_gain).astype(jnp.bfloat16)
    upstream = out_cotangent.astype(jnp.float32) * text_gain
    cross_mean = lax.optimization_barrier(jnp.mean(upstream * hidden_wide, axis=1, keepdims=True))
    hidden_grad = (hidden_inv * (upstream - hidden_wide * hidden_inv * hidden_inv * cross_mean)).astype(jnp.bfloat16)
    source = jnp.where(live_rows, slot_of_row, 0).astype(jnp.int32)
    feature_grad = jnp.where(live_rows[:, None], hidden_grad[source], jnp.zeros((), jnp.bfloat16))
    projected_grad = (feature_grad.astype(jnp.float32) * gelu_slope(projected)).astype(jnp.bfloat16)
    normed_grad = jnp.dot(projected_grad, proj_weight.T, preferred_element_type=jnp.float32)
    weighted = normed_grad * vision_gain
    weighted_mean = lax.optimization_barrier(jnp.mean(weighted, axis=1, keepdims=True))
    vision_cross = lax.optimization_barrier(jnp.mean(weighted * vision_hat, axis=1, keepdims=True))
    vision_grad = vision_inv * (weighted - weighted_mean - vision_hat * vision_cross)
    return (normed, vision_grad.astype(jnp.bfloat16))
```

```python
import jax
import jax.numpy as jnp
from jax import lax
from jax.sharding import PartitionSpec as P

D = 4096
UNIT = 16


VISION_EPS = 1e-05
EPSILON = 1e-06
HALF_ROOT = 0.7071067811865476
INV_ROOT_TWO_PI = 0.3989422804014327


def gelu_value(values):
    return 0.5 * values * (1.0 + lax.erf(values * HALF_ROOT))


def gelu_slope(values):
    return (
        0.5 * (1.0 + lax.erf(values * HALF_ROOT))
        + values * jnp.exp(-0.5 * values * values) * INV_ROOT_TWO_PI
    )


def shards(
    vision_rows,
    vision_gain,
    vision_bias,
    proj_weight,
    text_rows,
    text_gain,
    slot_of_row,
    out_cotangent,
):
    sections = lax.axis_size("section")
    groups = lax.axis_size("dp")
    tensor_count = lax.axis_size("tensor")
    row_total = vision_rows.shape[0]
    lang_total = text_rows.shape[0]
    column_count = text_rows.shape[1]
    unit_total = row_total // UNIT
    lang_units = lang_total // UNIT
    capacity = unit_total // sections
    bucket_count = sections * capacity
    column_total = vision_rows.shape[1]
    depth = proj_weight.shape[0]
    parts = sections * groups
    share = row_total // tensor_count
    share_start = lax.axis_index("tensor") * share
    own_rows = lax.dynamic_slice_in_dim(vision_rows, share_start, share, 0)
    vision_wide = own_rows.astype(jnp.float32)
    centered = vision_wide - jnp.mean(vision_wide, axis=1, keepdims=True)
    own_inv = lax.rsqrt(jnp.mean(centered * centered, axis=1, keepdims=True) + VISION_EPS)
    own_hat = centered * own_inv
    normed_vision = (own_hat * vision_gain + vision_bias).astype(jnp.bfloat16)
    outgoing = normed_vision.reshape(share, parts, depth).transpose(1, 0, 2)
    incoming = lax.all_to_all(
        outgoing, ("section", "dp"), split_axis=0, concat_axis=0, tiled=True
    )
    rows_all = lax.all_gather(incoming, "tensor", axis=1, tiled=True)
    rows_all = rows_all.reshape(parts * row_total, depth)
    partial_out = jnp.dot(rows_all, proj_weight, preferred_element_type=jnp.float32)
    projected = lax.psum_scatter(
        partial_out.astype(jnp.bfloat16), ("section", "dp"), scatter_dimension=0, tiled=True
    ).astype(jnp.float32)
    features = gelu_value(projected).astype(jnp.bfloat16)
    unit_slot = slot_of_row.reshape(unit_total, UNIT)[:, 0]
    unit_live = unit_slot >= 0
    target_device = jnp.where(unit_live, unit_slot // lang_total, 0) // groups
    same_target = (
        (target_device[:, None] == target_device[None, :]) & unit_live[:, None] & unit_live[None, :]
    )
    unit_order = jnp.arange(unit_total)
    earlier = unit_order[None, :] < unit_order[:, None]
    unit_rank = jnp.sum((same_target & earlier).astype(jnp.int32), axis=1)
    bucket = jnp.clip(target_device * capacity + unit_rank, 0, bucket_count - 1)
    chosen = (jnp.arange(bucket_count)[:, None] == bucket[None, :]) & unit_live[None, :]
    chosen_int = chosen.astype(jnp.int32)
    bucket_used = jnp.sum(chosen_int, axis=1) > 0
    bucket_source = jnp.sum(chosen_int * unit_order[None, :], axis=1)
    feature_units = features.reshape(unit_total, UNIT * column_count)
    send_rows = jnp.where(
        bucket_used[:, None], feature_units[bucket_source], jnp.zeros((), jnp.bfloat16)
    )
    send_slots = jnp.where(bucket_used, jnp.sum(chosen_int * unit_slot[None, :], axis=1), -1)
    arrived, arrived_slots = (
        lax.all_to_all(
            send_rows.reshape(sections, capacity * UNIT, column_count),
            "section",
            split_axis=0,
            concat_axis=0,
            tiled=True,
        ),
        lax.all_to_all(
            send_slots.reshape(sections, capacity),
            "section",
            split_axis=0,
            concat_axis=0,
            tiled=True,
        ),
    )
    lang_index = lax.axis_index("section") * groups + lax.axis_index("dp")
    arrived_slots = arrived_slots.reshape(bucket_count)
    arrived_live = arrived_slots >= 0
    arrived_position = jnp.clip(
        (arrived_slots - lang_index * lang_total) // UNIT, 0, lang_units - 1
    )
    placement = (jnp.arange(lang_units)[:, None] == arrived_position[None, :]) & arrived_live[
        None, :
    ]
    placement_int = placement.astype(jnp.int32)
    slot_is_image = jnp.sum(placement_int, axis=1) > 0
    slot_source = jnp.sum(placement_int * jnp.arange(bucket_count)[None, :], axis=1)
    arrived_units = arrived.reshape(bucket_count, UNIT * column_count)
    hidden_units = jnp.where(
        slot_is_image[:, None],
        arrived_units[slot_source],
        text_rows.reshape(lang_units, UNIT * column_count),
    )
    hidden_wide = hidden_units.reshape(lang_total, column_count).astype(jnp.float32)
    upstream = out_cotangent.astype(jnp.float32) * text_gain
    sums = jnp.stack(
        [jnp.sum(hidden_wide * hidden_wide, axis=1), jnp.sum(upstream * hidden_wide, axis=1)]
    )
    square_total, cross_total = lax.psum(sums, "tensor")
    hidden_inv = lax.rsqrt(square_total / D + EPSILON)[:, None]
    normed = (hidden_wide * hidden_inv * text_gain).astype(jnp.bfloat16)
    cross_mean = (cross_total / D)[:, None]
    hidden_grad = (
        hidden_inv * (upstream - hidden_wide * hidden_inv * hidden_inv * cross_mean)
    ).astype(jnp.bfloat16)
    grad_units = hidden_grad.reshape(lang_units, UNIT * column_count)
    reply_rows = jnp.where(
        arrived_live[:, None], grad_units[arrived_position], jnp.zeros((), jnp.bfloat16)
    )
    returned = lax.all_to_all(
        reply_rows.reshape(sections, capacity * UNIT, column_count),
        "section",
        split_axis=0,
        concat_axis=0,
        tiled=True,
    )
    returned_units = returned.reshape(bucket_count, UNIT * column_count)
    feature_grad = jnp.where(
        unit_live[:, None], returned_units[bucket], jnp.zeros((), jnp.bfloat16)
    )
    feature_grad = feature_grad.reshape(row_total, column_count)
    projected_grad = (feature_grad.astype(jnp.float32) * gelu_slope(projected)).astype(jnp.bfloat16)
    grad_all = lax.all_gather(projected_grad, ("section", "dp"), axis=0, tiled=True)
    contract_dims = (((1,), (1,)), ((), ()))
    partial_grad = lax.dot_general(
        grad_all, proj_weight, contract_dims, preferred_element_type=jnp.float32
    )
    partial_grad = partial_grad.astype(jnp.bfloat16).reshape(parts, row_total, depth)
    summed = lax.psum_scatter(partial_grad, "tensor", scatter_dimension=1, tiled=True)
    gathered = lax.all_to_all(
        summed, ("section", "dp"), split_axis=0, concat_axis=0, tiled=True
    )
    normed_grad = gathered.transpose(1, 0, 2).reshape(share, column_total).astype(jnp.float32)
    weighted = normed_grad * vision_gain
    weighted_mean = jnp.mean(weighted, axis=1, keepdims=True)
    vision_cross = jnp.mean(weighted * own_hat, axis=1, keepdims=True)
    vision_grad = own_inv * (weighted - weighted_mean - own_hat * vision_cross)
    return (normed, vision_grad.astype(jnp.bfloat16))


def solution(mesh):
    in_specs = (
        P(("section", "dp"), None),
        P(),
        P(),
        P(("section", "dp"), "tensor"),
        P(("section", "dp"), "tensor"),
        P("tensor"),
        P(("section", "dp")),
        P(("section", "dp"), "tensor"),
    )
    out_specs = (P(("section", "dp"), "tensor"), P(("section", "dp", "tensor"), None))
    return jax.shard_map(shards, mesh=mesh, in_specs=in_specs, out_specs=out_specs, check_vma=False)
```

```python
import functools

import jax
import jax.numpy as jnp
from jax import lax
from jax.experimental import pallas as pl
from jax.experimental.pallas import tpu as pltpu
from jax.sharding import PartitionSpec as P

D = 4096
UNIT = 16


VISION_EPS = 1e-05
EPSILON = 1e-06
HALF_ROOT = 0.7071067811865476
INV_ROOT_TWO_PI = 0.3989422804014327


def gelu_value(values):
    return 0.5 * values * (1.0 + lax.erf(values * HALF_ROOT))


def gelu_slope(values):
    return (
        0.5 * (1.0 + lax.erf(values * HALF_ROOT))
        + values * jnp.exp(-0.5 * values * values) * INV_ROOT_TWO_PI
    )


MESH = pl.DeviceIdType.MESH
BF16 = jnp.bfloat16
F32 = jnp.float32


def exchange_kernel(
    sections,
    groups,
    tensor_count,
    x_in,
    weight,
    text,
    gain,
    slots_row,
    slots_col,
    cotangent,
    normed_out,
    grad_out,
    x_all,
    own,
    part_send,
    part_recv,
    group_send,
    group_recv,
    slope,
    features,
    slots_all,
    stats,
    grads,
    pg_all,
    grad_part,
    keep,
    core_send,
    core_recv,
    y_send,
    y_recv,
    last_send,
    last_recv,
    x_ssem,
    x_rsem,
    fwd_ssem,
    part_ssem,
    part_rsem,
    group_ssem,
    group_rsem,
    feat_ssem,
    feat_rsem,
    slot_ssem,
    slot_rsem,
    stat_ssem,
    stat_rsem,
    grad_ssem,
    grad_rsem,
    pgz_ssem,
    pgx_ssem,
    pg_rsem,
    core_ssem,
    core_rsem,
    y_ssem,
    y_rsem,
    last_ssem,
    last_rsem,
):
    S, G, T = sections, groups, tensor_count
    N, Y = S * G, T // 2
    s = lax.axis_index("section")
    d = lax.axis_index("dp")
    t = lax.axis_index("tensor")
    y, c = t // 2, t % 2
    me = s * G + d
    mate = y * 2 + 1 - c
    share, depth = x_in.shape[1], x_in.shape[2]
    rows, cols = share * T, weight.shape[1]
    lang = text.shape[0]

    def send(src, dst, ssem, rsem, device):
        pltpu.make_async_remote_copy(
            src_ref=src,
            dst_ref=dst,
            send_sem=ssem,
            recv_sem=rsem,
            device_id=device,
            device_id_type=MESH,
        ).start()

    def arrived(ref, sem):
        pltpu.make_async_copy(ref, ref, sem).wait()

    def loop(count, body):
        def step(i, carry):
            body(i)
            return carry

        lax.fori_loop(0, count, step, 0)

    barrier = pltpu.get_barrier_semaphore()

    def greet(i):
        @pl.when(i != me)
        def _():
            pl.semaphore_signal(barrier, inc=1, device_id=(i // G, i % G, t), device_id_type=MESH)

    loop(N, greet)
    for dt in range(1, T):
        pl.semaphore_signal(barrier, inc=1, device_id=(s, d, (t + dt) % T), device_id_type=MESH)
    pl.semaphore_wait(barrier, N - 1 + T - 1)

    def send_x(j):
        to_s, to_d = (s + j % S + 1) % S, (d + j // S + 1) % G
        k = to_s * G + to_d

        @pl.when(k != me)
        def _():
            send(x_in.at[k], x_all.at[t, me], x_ssem.at[k], x_rsem.at[t, me], (to_s, to_d, t))

    loop(N, send_x)
    x_all[t, me] = x_in[me]

    def forward_x(j):
        k = ((s - j % S - 1 + S) % S) * G + (d - j // S - 1 + G) % G

        @pl.when(k != me)
        def _():
            arrived(x_all.at[t, k], x_rsem.at[t, k])

        block = x_all.at[t, k]
        for dy in range(1, Y):
            peer = ((y + dy) % Y) * 2 + c
            send(block, block, fwd_ssem.at[dy, k], x_rsem.at[t, k], (s, d, peer))
        send(block, block, fwd_ssem.at[0, k], x_rsem.at[t, k], (s, d, mate))

    loop(N, forward_x)

    def combine_group(j):
        at_d = (d - j - 1 + G) % G
        total = own[at_d]
        for js in range(1, S):
            arrived(part_recv.at[js - 1, at_d], part_rsem.at[js - 1, at_d])
            total = total + part_recv[js - 1, at_d].astype(F32)

        own[at_d] = total

        @pl.when(j < G - 1)
        def _():
            group_send[at_d] = total.astype(BF16)
            slot = (d - at_d + G) % G - 1
            send(
                group_send.at[at_d],
                group_recv.at[slot],
                group_ssem.at[at_d],
                group_rsem.at[slot],
                (s, at_d, t),
            )

    def project_group(j):
        at_d = (d - j - 1 + G) % G

        def project_block(i):
            at_s = (s - i - 1 + S) % S
            k = at_s * G + at_d
            for dy in range(1, Y):
                other = ((y + dy) % Y) * 2 + c
                block = x_all.at[other, k]
                arrived(block, x_rsem.at[other, k])
                send(block, block, fwd_ssem.at[Y - 1 + dy, k], x_rsem.at[other, k], (s, d, mate))
            for at_y in range(Y):
                other = at_y * 2 + 1 - c
                arrived(x_all.at[other, k], x_rsem.at[other, k])
            block = x_all[:, k].reshape(rows, depth)
            partial_out = jnp.dot(block, weight[...], preferred_element_type=F32)

            @pl.when(at_s == s)
            def _():
                own[at_d] = partial_out

            @pl.when(at_s != s)
            def _():
                part_send[k] = partial_out.astype(BF16)
                slot = (s - at_s + S) % S - 1
                send(
                    part_send.at[k],
                    part_recv.at[slot, at_d],
                    part_ssem.at[k],
                    part_rsem.at[slot, at_d],
                    (at_s, d, t),
                )

        loop(S, project_block)

    def project_step(j):
        @pl.when(j < G)
        def _():
            project_group(j)

        @pl.when(j > 0)
        def _():
            combine_group(j - 1)

    loop(G + 1, project_step)

    projected = own[d]
    for slot in range(G - 1):
        arrived(group_recv.at[slot], group_rsem.at[slot])
        projected = projected + group_recv[slot].astype(F32)
    features[0] = gelu_value(projected).astype(BF16)
    slots_all[0] = slots_row[...]
    for js in range(1, S):
        peer = ((s + js) % S, d, t)
        send(features.at[0], features.at[S - js], feat_ssem.at[js], feat_rsem.at[S - js], peer)
        send(slots_row, slots_all.at[S - js], slot_ssem.at[js], slot_rsem.at[S - js], peer)
    slope[...] = gelu_slope(projected)
    for js in range(1, S):
        arrived(features.at[js], feat_rsem.at[js])
        arrived(slots_all.at[js], slot_rsem.at[js])

    slot_ids = me * lang + lax.broadcasted_iota(jnp.int32, (lang, rows), 0)
    placed = jnp.zeros((lang, cols), F32)
    taken = jnp.zeros((lang, 1), F32)
    for js in range(S):
        chosen = jnp.where(slots_all[js][0:1, :] == slot_ids, 1.0, 0.0)
        taken = taken + jnp.sum(chosen, axis=1, keepdims=True)
        placed = placed + jnp.dot(
            chosen.astype(BF16), features[js], preferred_element_type=F32
        )
    hidden = jnp.where(taken > 0.5, placed, text[...].astype(F32))
    upstream = cotangent[...].astype(F32) * gain[...]
    squares = jnp.sum(hidden * hidden, axis=1, keepdims=True)
    crosses = jnp.sum(upstream * hidden, axis=1, keepdims=True)
    lanes = lax.broadcasted_iota(jnp.int32, (lang, 128), 1)
    stats[0] = jnp.where(lanes < 64, squares, crosses)
    for dt in range(1, T):
        peer = (s, d, (t + dt) % T)
        send(stats.at[0], stats.at[T - dt], stat_ssem.at[dt], stat_rsem.at[T - dt], peer)
    total = stats[0]
    for dt in range(1, T):
        arrived(stats.at[dt], stat_rsem.at[dt])
        total = total + stats[dt]
    hidden_inv = lax.rsqrt(total[:, 0:1] / D + EPSILON)
    cross_mean = total[:, 64:65] / D
    grads[0] = (
        hidden_inv * (upstream - hidden * hidden_inv * hidden_inv * cross_mean)
    ).astype(BF16)
    for js in range(1, S):
        peer = ((s + js) % S, d, t)
        send(grads.at[0], grads.at[S - js], grad_ssem.at[js], grad_rsem.at[S - js], peer)
    normed_out[...] = (hidden * hidden_inv * gain[...]).astype(BF16)

    feature_grad = jnp.zeros((rows, cols), F32)
    lane_ids = lax.broadcasted_iota(jnp.int32, (rows, lang), 1)
    for js in range(S):
        if js > 0:
            arrived(grads.at[js], grad_rsem.at[js])
        first = (((s + js) % S) * G + d) * lang
        chosen = jnp.where(slots_col[...] == first + lane_ids, 1.0, 0.0).astype(BF16)
        feature_grad = feature_grad + jnp.dot(chosen, grads[js], preferred_element_type=F32)
    pg_all[me] = (feature_grad * slope[...]).astype(BF16)

    for jd in range(1, G):
        send(
            pg_all.at[me],
            pg_all.at[me],
            pgz_ssem.at[jd],
            pg_rsem.at[me],
            (s, (d + jd) % G, t),
        )

    def reduce_cores(k):
        arrived(core_recv.at[k], core_rsem.at[k])
        for at_y in range(Y):
            keep[k, at_y] = keep[k, at_y] + core_recv[k, at_y].astype(F32)
        for dy in range(1, Y):
            to_y = (y + dy) % Y
            y_send[k, dy - 1] = keep[k, to_y].astype(BF16)
            send(
                y_send.at[k, dy - 1],
                y_recv.at[k, Y - dy - 1],
                y_ssem.at[k, dy - 1],
                y_rsem.at[k, Y - dy - 1],
                (s, d, to_y * 2 + c),
            )

    def spread_step(j):
        at_d = (d - j + G) % G
        mine = s * G + at_d

        @pl.when(j < G)
        def _():
            @pl.when(j > 0)
            def _():
                arrived(pg_all.at[mine], pg_rsem.at[mine])

            for js in range(1, S):
                send(
                    pg_all.at[mine],
                    pg_all.at[mine],
                    pgx_ssem.at[js, at_d],
                    pg_rsem.at[mine],
                    ((s + js) % S, d, t),
                )

            def back_block(i):
                k = ((s + i) % S) * G + at_d

                @pl.when(i > 0)
                def _():
                    arrived(pg_all.at[k], pg_rsem.at[k])

                grad_part[...] = lax.dot_general(
                    pg_all[k], weight[...], (((1,), (1,)), ((), ())), preferred_element_type=F32
                ).reshape(Y, 2, share, depth)
                for at_y in range(Y):
                    keep[k, at_y] = grad_part[at_y, c]
                    core_send[k, at_y] = grad_part[at_y, 1 - c].astype(BF16)
                send(
                    core_send.at[k], core_recv.at[k], core_ssem.at[k], core_rsem.at[k], (s, d, mate)
                )

            loop(S, back_block)

        @pl.when(j > 0)
        def _():
            before = (d - j + 1 + G) % G
            loop(S, lambda i: reduce_cores(((s + i) % S) * G + before))

    loop(G + 1, spread_step)

    def finish(j):
        to_s, to_d = (s + j % S) % S, (d - j // S + G) % G
        k = to_s * G + to_d
        total = keep[k, y]
        for dy in range(1, Y):
            arrived(y_recv.at[k, dy - 1], y_rsem.at[k, dy - 1])
            total = total + y_recv[k, dy - 1].astype(F32)
        last_send[k] = total.astype(BF16)

        @pl.when(k != me)
        def _():
            send(
                last_send.at[k], last_recv.at[me], last_ssem.at[k], last_rsem.at[me], (to_s, to_d, t)
            )

    loop(N, finish)

    def collect(k):
        @pl.when(k != me)
        def _():
            arrived(last_recv.at[k], last_rsem.at[k])
            grad_out[k] = last_recv[k]
            arrived(last_send.at[k], last_ssem.at[k])
            arrived(x_in.at[k], x_ssem.at[k])

        for i in range(2 * Y - 1):
            arrived(x_all.at[t, k], fwd_ssem.at[i, k])
        arrived(core_send.at[k], core_ssem.at[k])
        for dy in range(1, Y):
            arrived(y_send.at[k, dy - 1], y_ssem.at[k, dy - 1])

        @pl.when(k // G != s)
        def _():
            arrived(part_send.at[k], part_ssem.at[k])

    grad_out[me] = last_send[me]
    loop(N, collect)

    def drain(k):
        @pl.when(k != d)
        def _():
            arrived(group_send.at[k], group_ssem.at[k])

        for js in range(1, S):
            arrived(pg_all.at[me], pgx_ssem.at[js, k])

    loop(G, drain)
    for jd in range(1, G):
        arrived(pg_all.at[me], pgz_ssem.at[jd])
    for js in range(1, S):
        arrived(features.at[0], feat_ssem.at[js])
        arrived(slots_row, slot_ssem.at[js])
        arrived(grads.at[0], grad_ssem.at[js])
    for dt in range(1, T):
        arrived(stats.at[0], stat_ssem.at[dt])


def exchange(S, G, T, x_in, weight, text, gain, slots, cotangent):
    N, Y = S * G, T // 2
    share, depth = x_in.shape[1:]
    rows = share * T
    lang, cols = text.shape
    slots_row = jnp.broadcast_to(slots[None, :], (8, rows))
    slots_col = jnp.broadcast_to(slots[:, None], (rows, lang))
    sem = pltpu.SemaphoreType.DMA
    vmem = pltpu.VMEM
    whole = pl.BlockSpec(memory_space=pltpu.VMEM)
    return pl.pallas_call(
        functools.partial(exchange_kernel, S, G, T),
        out_shape=(
            jax.ShapeDtypeStruct((lang, cols), BF16),
            jax.ShapeDtypeStruct((N, share, depth), BF16),
        ),
        in_specs=[whole] * 7,
        out_specs=(whole, whole),
        scratch_shapes=[
            vmem((T, N, share, depth), BF16),
            vmem((G, rows, cols), F32),
            vmem((N, rows, cols), BF16),
            vmem((S - 1, G, rows, cols), BF16),
            vmem((G, rows, cols), BF16),
            vmem((G - 1, rows, cols), BF16),
            vmem((rows, cols), F32),
            vmem((S, rows, cols), BF16),
            vmem((S, 8, rows), jnp.int32),
            vmem((T, lang, 128), F32),
            vmem((S, lang, cols), BF16),
            vmem((N, rows, cols), BF16),
            vmem((Y, 2, share, depth), F32),
            vmem((N, Y, share, depth), F32),
            vmem((N, Y, share, depth), BF16),
            vmem((N, Y, share, depth), BF16),
            vmem((N, Y - 1, share, depth), BF16),
            vmem((N, Y - 1, share, depth), BF16),
            vmem((N, share, depth), BF16),
            vmem((N, share, depth), BF16),
            sem((N,)),
            sem((T, N)),
            sem((2 * Y - 1, N)),
            sem((N,)),
            sem((S - 1, G)),
            sem((G,)),
            sem((G - 1,)),
            sem((S,)),
            sem((S,)),
            sem((S,)),
            sem((S,)),
            sem((T,)),
            sem((T,)),
            sem((S,)),
            sem((S,)),
            sem((G,)),
            sem((S, G)),
            sem((N,)),
            sem((N,)),
            sem((N,)),
            sem((N, Y - 1)),
            sem((N, Y - 1)),
            sem((N,)),
            sem((N,)),
        ],
        compiler_params=pltpu.CompilerParams(
            collective_id=0, has_side_effects=True, vmem_limit_bytes=58 * 1024 * 1024
        ),
        cost_estimate=pl.CostEstimate(
            flops=4 * N * rows * depth * cols, bytes_accessed=16 * 1024 * 1024, transcendentals=0
        ),
    )(x_in, weight, text, gain[None, :], slots_row, slots_col, cotangent)


def vision_backward(gathered, vision_gain, own_hat, own_inv):
    normed_grad = gathered.transpose(1, 0, 2).reshape(own_hat.shape).astype(jnp.float32)
    weighted = normed_grad * vision_gain
    weighted_mean = jnp.mean(weighted, axis=1, keepdims=True)
    vision_cross = jnp.mean(weighted * own_hat, axis=1, keepdims=True)
    vision_grad = own_inv * (weighted - weighted_mean - own_hat * vision_cross)
    return vision_grad.astype(jnp.bfloat16)


def shards(
    vision_rows,
    vision_gain,
    vision_bias,
    proj_weight,
    text_rows,
    text_gain,
    slot_of_row,
    out_cotangent,
):
    sections = lax.axis_size("section")
    groups = lax.axis_size("dp")
    tensor_count = lax.axis_size("tensor")
    row_total = vision_rows.shape[0]
    lang_total = text_rows.shape[0]
    column_count = text_rows.shape[1]
    unit_total = row_total // UNIT
    lang_units = lang_total // UNIT
    capacity = unit_total // sections
    bucket_count = sections * capacity
    column_total = vision_rows.shape[1]
    depth = proj_weight.shape[0]
    parts = sections * groups
    share = row_total // tensor_count
    share_start = lax.axis_index("tensor") * share
    own_rows = lax.dynamic_slice_in_dim(vision_rows, share_start, share, 0)
    vision_wide = own_rows.astype(jnp.float32)
    centered = vision_wide - jnp.mean(vision_wide, axis=1, keepdims=True)
    own_inv = lax.rsqrt(jnp.mean(centered * centered, axis=1, keepdims=True) + VISION_EPS)
    own_hat = centered * own_inv
    normed_vision = (own_hat * vision_gain + vision_bias).astype(jnp.bfloat16)
    outgoing = normed_vision.reshape(share, parts, depth).transpose(1, 0, 2)
    if min(sections, groups) > 1 and parts <= 8 and tensor_count == 4 and lang_total % 128 == 0:
        normed, gathered = exchange(
            sections,
            groups,
            tensor_count,
            outgoing,
            proj_weight,
            text_rows,
            text_gain,
            slot_of_row,
            out_cotangent,
        )
        return normed, vision_backward(gathered, vision_gain, own_hat, own_inv)
    incoming = lax.all_to_all(
        outgoing, ("section", "dp"), split_axis=0, concat_axis=0, tiled=True
    )
    rows_all = lax.all_gather(incoming, "tensor", axis=1, tiled=True)
    rows_all = rows_all.reshape(parts * row_total, depth)
    partial_out = jnp.dot(rows_all, proj_weight, preferred_element_type=jnp.float32)
    projected = lax.psum_scatter(
        partial_out.astype(jnp.bfloat16), ("section", "dp"), scatter_dimension=0, tiled=True
    ).astype(jnp.float32)
    features = gelu_value(projected).astype(jnp.bfloat16)
    unit_slot = slot_of_row.reshape(unit_total, UNIT)[:, 0]
    unit_live = unit_slot >= 0
    target_device = jnp.where(unit_live, unit_slot // lang_total, 0) // groups
    same_target = (
        (target_device[:, None] == target_device[None, :]) & unit_live[:, None] & unit_live[None, :]
    )
    unit_order = jnp.arange(unit_total)
    earlier = unit_order[None, :] < unit_order[:, None]
    unit_rank = jnp.sum((same_target & earlier).astype(jnp.int32), axis=1)
    bucket = jnp.clip(target_device * capacity + unit_rank, 0, bucket_count - 1)
    chosen = (jnp.arange(bucket_count)[:, None] == bucket[None, :]) & unit_live[None, :]
    chosen_int = chosen.astype(jnp.int32)
    bucket_used = jnp.sum(chosen_int, axis=1) > 0
    bucket_source = jnp.sum(chosen_int * unit_order[None, :], axis=1)
    feature_units = features.reshape(unit_total, UNIT * column_count)
    send_rows = jnp.where(
        bucket_used[:, None], feature_units[bucket_source], jnp.zeros((), jnp.bfloat16)
    )
    send_slots = jnp.where(bucket_used, jnp.sum(chosen_int * unit_slot[None, :], axis=1), -1)
    arrived, arrived_slots = (
        lax.all_to_all(
            send_rows.reshape(sections, capacity * UNIT, column_count),
            "section",
            split_axis=0,
            concat_axis=0,
            tiled=True,
        ),
        lax.all_to_all(
            send_slots.reshape(sections, capacity),
            "section",
            split_axis=0,
            concat_axis=0,
            tiled=True,
        ),
    )
    lang_index = lax.axis_index("section") * groups + lax.axis_index("dp")
    arrived_slots = arrived_slots.reshape(bucket_count)
    arrived_live = arrived_slots >= 0
    arrived_position = jnp.clip(
        (arrived_slots - lang_index * lang_total) // UNIT, 0, lang_units - 1
    )
    placement = (jnp.arange(lang_units)[:, None] == arrived_position[None, :]) & arrived_live[
        None, :
    ]
    placement_int = placement.astype(jnp.int32)
    slot_is_image = jnp.sum(placement_int, axis=1) > 0
    slot_source = jnp.sum(placement_int * jnp.arange(bucket_count)[None, :], axis=1)
    arrived_units = arrived.reshape(bucket_count, UNIT * column_count)
    hidden_units = jnp.where(
        slot_is_image[:, None],
        arrived_units[slot_source],
        text_rows.reshape(lang_units, UNIT * column_count),
    )
    hidden_wide = hidden_units.reshape(lang_total, column_count).astype(jnp.float32)
    upstream = out_cotangent.astype(jnp.float32) * text_gain
    sums = jnp.stack(
        [jnp.sum(hidden_wide * hidden_wide, axis=1), jnp.sum(upstream * hidden_wide, axis=1)]
    )
    square_total, cross_total = lax.psum(sums, "tensor")
    hidden_inv = lax.rsqrt(square_total / D + EPSILON)[:, None]
    normed = (hidden_wide * hidden_inv * text_gain).astype(jnp.bfloat16)
    cross_mean = (cross_total / D)[:, None]
    hidden_grad = (
        hidden_inv * (upstream - hidden_wide * hidden_inv * hidden_inv * cross_mean)
    ).astype(jnp.bfloat16)
    grad_units = hidden_grad.reshape(lang_units, UNIT * column_count)
    reply_rows = jnp.where(
        arrived_live[:, None], grad_units[arrived_position], jnp.zeros((), jnp.bfloat16)
    )
    returned = lax.all_to_all(
        reply_rows.reshape(sections, capacity * UNIT, column_count),
        "section",
        split_axis=0,
        concat_axis=0,
        tiled=True,
    )
    returned_units = returned.reshape(bucket_count, UNIT * column_count)
    feature_grad = jnp.where(
        unit_live[:, None], returned_units[bucket], jnp.zeros((), jnp.bfloat16)
    )
    feature_grad = feature_grad.reshape(row_total, column_count)
    projected_grad = (feature_grad.astype(jnp.float32) * gelu_slope(projected)).astype(jnp.bfloat16)
    grad_all = lax.all_gather(projected_grad, ("section", "dp"), axis=0, tiled=True)
    contract_dims = (((1,), (1,)), ((), ()))
    partial_grad = lax.dot_general(
        grad_all, proj_weight, contract_dims, preferred_element_type=jnp.float32
    )
    partial_grad = partial_grad.astype(jnp.bfloat16).reshape(parts, row_total, depth)
    summed = lax.psum_scatter(partial_grad, "tensor", scatter_dimension=1, tiled=True)
    gathered = lax.all_to_all(
        summed, ("section", "dp"), split_axis=0, concat_axis=0, tiled=True
    )
    return normed, vision_backward(gathered, vision_gain, own_hat, own_inv)


def solution(mesh):
    in_specs = (
        P(("section", "dp"), None),
        P(),
        P(),
        P(("section", "dp"), "tensor"),
        P(("section", "dp"), "tensor"),
        P("tensor"),
        P(("section", "dp")),
        P(("section", "dp"), "tensor"),
    )
    out_specs = (P(("section", "dp"), "tensor"), P(("section", "dp", "tensor"), None))
    return jax.shard_map(shards, mesh=mesh, in_specs=in_specs, out_specs=out_specs, check_vma=False)
```

```python
import functools

import jax
import jax.numpy as jnp
from jax import lax
from jax.experimental import pallas as pl
from jax.experimental.pallas import tpu as pltpu
from jax.sharding import PartitionSpec as P

D = 4096
UNIT = 16


VISION_EPS = 1e-05
EPSILON = 1e-06
HALF_ROOT = 0.7071067811865476
INV_ROOT_TWO_PI = 0.3989422804014327


def gelu_value(values):
    return 0.5 * values * (1.0 + lax.erf(values * HALF_ROOT))


def gelu_slope(values):
    return (
        0.5 * (1.0 + lax.erf(values * HALF_ROOT))
        + values * jnp.exp(-0.5 * values * values) * INV_ROOT_TWO_PI
    )


MESH = pl.DeviceIdType.MESH
BF16 = jnp.bfloat16
F32 = jnp.float32


def exchange_kernel(
    sections,
    groups,
    tensor_count,
    vision,
    vision_gain,
    vision_bias,
    weight,
    text,
    gain,
    slots,
    cotangent,
    normed_out,
    grad_out,
    raw,
    x_in,
    hat,
    inverse,
    slots_row,
    x_all,
    own,
    part_send,
    part_recv,
    group_send,
    group_recv,
    slope,
    features,
    slots_all,
    stats,
    grads,
    pg_all,
    grad_part,
    keep,
    core_send,
    core_recv,
    y_send,
    y_recv,
    last_send,
    last_recv,
    x_ssem,
    x_rsem,
    fwd_ssem,
    part_ssem,
    part_rsem,
    group_ssem,
    group_rsem,
    feat_ssem,
    feat_rsem,
    slot_ssem,
    slot_rsem,
    stat_ssem,
    stat_rsem,
    grad_ssem,
    grad_rsem,
    pgz_ssem,
    pgx_ssem,
    pg_rsem,
    core_ssem,
    core_rsem,
    y_ssem,
    y_rsem,
    last_ssem,
    last_rsem,
    raw_sem,
):
    S, G, T = sections, groups, tensor_count
    N, Y = S * G, T // 2
    s = lax.axis_index("section")
    d = lax.axis_index("dp")
    t = lax.axis_index("tensor")
    y, c = t // 2, t % 2
    me = s * G + d
    mate = y * 2 + 1 - c
    share, depth = x_in.shape[1], x_in.shape[2]
    column_total = vision.shape[1]
    rows, cols = share * T, weight.shape[1]
    lang = text.shape[0]

    def send(src, dst, ssem, rsem, device):
        pltpu.make_async_remote_copy(
            src_ref=src,
            dst_ref=dst,
            send_sem=ssem,
            recv_sem=rsem,
            device_id=device,
            device_id_type=MESH,
        ).start()

    def arrived(ref, sem):
        pltpu.make_async_copy(ref, ref, sem).wait()

    def loop(count, body):
        def step(i, carry):
            body(i)
            return carry

        lax.fori_loop(0, count, step, 0)

    barrier = pltpu.get_barrier_semaphore()

    def greet(i):
        @pl.when(i != me)
        def _():
            pl.semaphore_signal(barrier, inc=1, device_id=(i // G, i % G, t), device_id_type=MESH)

    fetch = pltpu.make_async_copy(vision.at[pl.ds(t * share, share)], raw, raw_sem)
    fetch.start()
    loop(N, greet)
    for dt in range(1, T):
        pl.semaphore_signal(barrier, inc=1, device_id=(s, d, (t + dt) % T), device_id_type=MESH)
    fetch.wait()
    sums = jnp.zeros((share, 128), F32)
    for at in range(0, column_total, 128):
        sums = sums + raw[:, at : at + 128].astype(F32)
    mean = jnp.sum(sums, axis=1, keepdims=True) / column_total
    sums = jnp.zeros((share, 128), F32)
    for at in range(0, column_total, 128):
        centered = raw[:, at : at + 128].astype(F32) - mean
        sums = sums + centered * centered
    square_mean = jnp.sum(sums, axis=1, keepdims=True) / column_total
    inverse[...] = jnp.broadcast_to(lax.rsqrt(square_mean + VISION_EPS), (share, 128))
    own_inv = inverse[:, 0:1]
    for n in range(N):
        span = slice(n * depth, (n + 1) * depth)
        own_hat = (raw[:, span].astype(F32) - mean) * own_inv
        hat[n] = own_hat
        x_in[n] = (own_hat * vision_gain[:, span] + vision_bias[:, span]).astype(BF16)
    slots_row[...] = jnp.broadcast_to(slots[...], (8, rows))
    pl.semaphore_wait(barrier, N - 1 + T - 1)

    def send_x(j):
        to_s, to_d = (s + j % S + 1) % S, (d + j // S + 1) % G
        k = to_s * G + to_d

        @pl.when(k != me)
        def _():
            send(x_in.at[k], x_all.at[t, me], x_ssem.at[k], x_rsem.at[t, me], (to_s, to_d, t))

    loop(N, send_x)
    x_all[t, me] = x_in[me]

    def forward_x(j):
        k = ((s - j % S - 1 + S) % S) * G + (d - j // S - 1 + G) % G

        @pl.when(k != me)
        def _():
            arrived(x_all.at[t, k], x_rsem.at[t, k])

        block = x_all.at[t, k]
        for dy in range(1, Y):
            peer = ((y + dy) % Y) * 2 + c
            send(block, block, fwd_ssem.at[dy, k], x_rsem.at[t, k], (s, d, peer))
        send(block, block, fwd_ssem.at[0, k], x_rsem.at[t, k], (s, d, mate))

    loop(N, forward_x)

    def combine_group(j):
        at_d = (d - j - 1 + G) % G
        total = own[at_d]
        for js in range(1, S):
            arrived(part_recv.at[js - 1, at_d], part_rsem.at[js - 1, at_d])
            total = total + part_recv[js - 1, at_d].astype(F32)

        own[at_d] = total

        @pl.when(j < G - 1)
        def _():
            group_send[at_d] = total.astype(BF16)
            slot = (d - at_d + G) % G - 1
            send(
                group_send.at[at_d],
                group_recv.at[slot],
                group_ssem.at[at_d],
                group_rsem.at[slot],
                (s, at_d, t),
            )

    def project_group(j):
        at_d = (d - j - 1 + G) % G

        def project_block(i):
            at_s = (s - i - 1 + S) % S
            k = at_s * G + at_d
            for dy in range(1, Y):
                other = ((y + dy) % Y) * 2 + c
                block = x_all.at[other, k]
                arrived(block, x_rsem.at[other, k])
                send(block, block, fwd_ssem.at[Y - 1 + dy, k], x_rsem.at[other, k], (s, d, mate))
            for at_y in range(Y):
                other = at_y * 2 + 1 - c
                arrived(x_all.at[other, k], x_rsem.at[other, k])
            block = x_all[:, k].reshape(rows, depth)
            partial_out = jnp.dot(block, weight[...], preferred_element_type=F32)

            @pl.when(at_s == s)
            def _():
                own[at_d] = partial_out

            @pl.when(at_s != s)
            def _():
                part_send[k] = partial_out.astype(BF16)
                slot = (s - at_s + S) % S - 1
                send(
                    part_send.at[k],
                    part_recv.at[slot, at_d],
                    part_ssem.at[k],
                    part_rsem.at[slot, at_d],
                    (at_s, d, t),
                )

        loop(S, project_block)

    def project_step(j):
        @pl.when(j < G)
        def _():
            project_group(j)

        @pl.when(j > 0)
        def _():
            combine_group(j - 1)

    loop(G + 1, project_step)

    projected = own[d]
    for slot in range(G - 1):
        arrived(group_recv.at[slot], group_rsem.at[slot])
        projected = projected + group_recv[slot].astype(F32)
    features[0] = gelu_value(projected).astype(BF16)
    slots_all[0] = slots_row[...]
    for js in range(1, S):
        peer = ((s + js) % S, d, t)
        send(features.at[0], features.at[S - js], feat_ssem.at[js], feat_rsem.at[S - js], peer)
        send(slots_row, slots_all.at[S - js], slot_ssem.at[js], slot_rsem.at[S - js], peer)
    slope[...] = gelu_slope(projected)
    for js in range(1, S):
        arrived(features.at[js], feat_rsem.at[js])
        arrived(slots_all.at[js], slot_rsem.at[js])

    slot_ids = me * lang + lax.broadcasted_iota(jnp.int32, (lang, rows), 0)
    placed = jnp.zeros((lang, cols), F32)
    taken = jnp.zeros((lang, 1), F32)
    for js in range(S):
        chosen = jnp.where(slots_all[js][0:1, :] == slot_ids, 1.0, 0.0)
        taken = taken + jnp.sum(chosen, axis=1, keepdims=True)
        placed = placed + jnp.dot(
            chosen.astype(BF16), features[js], preferred_element_type=F32
        )
    hidden = jnp.where(taken > 0.5, placed, text[...].astype(F32))
    upstream = cotangent[...].astype(F32) * gain[...]
    squares = jnp.sum(hidden * hidden, axis=1, keepdims=True)
    crosses = jnp.sum(upstream * hidden, axis=1, keepdims=True)
    lanes = lax.broadcasted_iota(jnp.int32, (lang, 128), 1)
    stats[0] = jnp.where(lanes % 8 < 4, squares, crosses).T[0:8]
    for dt in range(1, T):
        peer = (s, d, (t + dt) % T)
        send(stats.at[0], stats.at[T - dt], stat_ssem.at[dt], stat_rsem.at[T - dt], peer)
    total = stats[0]
    for dt in range(1, T):
        arrived(stats.at[dt], stat_rsem.at[dt])
        total = total + stats[dt]
    total = jnp.concatenate([total] * (128 // 8), axis=0).T
    hidden_inv = lax.rsqrt(total[:, 0:1] / D + EPSILON)
    cross_mean = total[:, 4:5] / D
    grads[0] = (
        hidden_inv * (upstream - hidden * hidden_inv * hidden_inv * cross_mean)
    ).astype(BF16)
    for js in range(1, S):
        peer = ((s + js) % S, d, t)
        send(grads.at[0], grads.at[S - js], grad_ssem.at[js], grad_rsem.at[S - js], peer)
    normed_out[...] = (hidden * hidden_inv * gain[...]).astype(BF16)

    feature_grad = jnp.zeros((rows, cols), F32)
    lane_ids = lax.broadcasted_iota(jnp.int32, (rows, lang), 1)
    slots_col = jnp.broadcast_to(slots[...], (rows, rows)).T
    for js in range(S):
        if js > 0:
            arrived(grads.at[js], grad_rsem.at[js])
        first = (((s + js) % S) * G + d) * lang
        chosen = jnp.where(slots_col == first + lane_ids, 1.0, 0.0).astype(BF16)
        feature_grad = feature_grad + jnp.dot(chosen, grads[js], preferred_element_type=F32)
    pg_all[me] = (feature_grad * slope[...]).astype(BF16)

    for jd in range(1, G):
        send(
            pg_all.at[me],
            pg_all.at[me],
            pgz_ssem.at[jd],
            pg_rsem.at[me],
            (s, (d + jd) % G, t),
        )

    def reduce_cores(k):
        arrived(core_recv.at[k], core_rsem.at[k])
        for at_y in range(Y):
            keep[k, at_y] = keep[k, at_y] + core_recv[k, at_y].astype(F32)
        for dy in range(1, Y):
            to_y = (y + dy) % Y
            y_send[k, dy - 1] = keep[k, to_y].astype(BF16)
            send(
                y_send.at[k, dy - 1],
                y_recv.at[k, Y - dy - 1],
                y_ssem.at[k, dy - 1],
                y_rsem.at[k, Y - dy - 1],
                (s, d, to_y * 2 + c),
            )

    def spread_step(j):
        at_d = (d - j + G) % G
        mine = s * G + at_d

        @pl.when(j < G)
        def _():
            @pl.when(j > 0)
            def _():
                arrived(pg_all.at[mine], pg_rsem.at[mine])

            for js in range(1, S):
                send(
                    pg_all.at[mine],
                    pg_all.at[mine],
                    pgx_ssem.at[js, at_d],
                    pg_rsem.at[mine],
                    ((s + js) % S, d, t),
                )

            def back_block(i):
                k = ((s + i) % S) * G + at_d

                @pl.when(i > 0)
                def _():
                    arrived(pg_all.at[k], pg_rsem.at[k])

                grad_part[...] = lax.dot_general(
                    pg_all[k], weight[...], (((1,), (1,)), ((), ())), preferred_element_type=F32
                ).reshape(Y, 2, share, depth)
                for at_y in range(Y):
                    keep[k, at_y] = grad_part[at_y, c]
                    core_send[k, at_y] = grad_part[at_y, 1 - c].astype(BF16)
                send(
                    core_send.at[k], core_recv.at[k], core_ssem.at[k], core_rsem.at[k], (s, d, mate)
                )

            loop(S, back_block)

        @pl.when(j > 0)
        def _():
            before = (d - j + 1 + G) % G
            loop(S, lambda i: reduce_cores(((s + i) % S) * G + before))

    loop(G + 1, spread_step)

    def finish(j):
        to_s, to_d = (s + j % S) % S, (d - j // S + G) % G
        k = to_s * G + to_d
        total = keep[k, y]
        for dy in range(1, Y):
            arrived(y_recv.at[k, dy - 1], y_rsem.at[k, dy - 1])
            total = total + y_recv[k, dy - 1].astype(F32)
        last_send[k] = total.astype(BF16)

        @pl.when(k != me)
        def _():
            send(
                last_send.at[k], last_recv.at[me], last_ssem.at[k], last_rsem.at[me], (to_s, to_d, t)
            )

    loop(N, finish)

    def collect(k):
        @pl.when(k != me)
        def _():
            arrived(last_recv.at[k], last_rsem.at[k])
            arrived(last_send.at[k], last_ssem.at[k])
            arrived(x_in.at[k], x_ssem.at[k])

        for i in range(2 * Y - 1):
            arrived(x_all.at[t, k], fwd_ssem.at[i, k])
        arrived(core_send.at[k], core_ssem.at[k])
        for dy in range(1, Y):
            arrived(y_send.at[k, dy - 1], y_ssem.at[k, dy - 1])

        @pl.when(k // G != s)
        def _():
            arrived(part_send.at[k], part_ssem.at[k])

    last_recv[me] = last_send[me]
    loop(N, collect)
    plain = jnp.zeros((share, 1), F32)
    crossed = jnp.zeros((share, 1), F32)
    for n in range(N):
        span = slice(n * depth, (n + 1) * depth)
        weighted = last_recv[n].astype(F32) * vision_gain[:, span]
        plain = plain + jnp.sum(weighted, axis=1, keepdims=True)
        crossed = crossed + jnp.sum(weighted * hat[n], axis=1, keepdims=True)
    plain = plain / column_total
    crossed = crossed / column_total
    own_inv = inverse[:, 0:1]
    for n in range(N):
        span = slice(n * depth, (n + 1) * depth)
        weighted = last_recv[n].astype(F32) * vision_gain[:, span]
        grad_out[:, span] = (own_inv * (weighted - plain - hat[n] * crossed)).astype(BF16)

    def drain(k):
        @pl.when(k != d)
        def _():
            arrived(group_send.at[k], group_ssem.at[k])

        for js in range(1, S):
            arrived(pg_all.at[me], pgx_ssem.at[js, k])

    loop(G, drain)
    for jd in range(1, G):
        arrived(pg_all.at[me], pgz_ssem.at[jd])
    for js in range(1, S):
        arrived(features.at[0], feat_ssem.at[js])
        arrived(slots_row, slot_ssem.at[js])
        arrived(grads.at[0], grad_ssem.at[js])
    for dt in range(1, T):
        arrived(stats.at[0], stat_ssem.at[dt])


def exchange(
    S, G, T, vision, vision_gain, vision_bias, weight, text, gain, slots, cotangent
):
    N, Y = S * G, T // 2
    rows, column_total = vision.shape
    share, depth = rows // T, weight.shape[0]
    lang, cols = text.shape
    sem = pltpu.SemaphoreType.DMA
    vmem = pltpu.VMEM
    whole = pl.BlockSpec(memory_space=pltpu.VMEM)
    return pl.pallas_call(
        functools.partial(exchange_kernel, S, G, T),
        out_shape=(
            jax.ShapeDtypeStruct((lang, cols), BF16),
            jax.ShapeDtypeStruct((share, column_total), BF16),
        ),
        in_specs=[pl.BlockSpec(memory_space=pl.ANY)] + [whole] * 7,
        out_specs=(whole, whole),
        scratch_shapes=[
            vmem((share, column_total), BF16),
            vmem((N, share, depth), BF16),
            vmem((N, share, depth), F32),
            vmem((share, 128), F32),
            vmem((8, rows), jnp.int32),
            vmem((T, N, share, depth), BF16),
            vmem((G, rows, cols), F32),
            vmem((N, rows, cols), BF16),
            vmem((S - 1, G, rows, cols), BF16),
            vmem((G, rows, cols), BF16),
            vmem((G - 1, rows, cols), BF16),
            vmem((rows, cols), F32),
            vmem((S, rows, cols), BF16),
            vmem((S, 8, rows), jnp.int32),
            vmem((T, 8, lang), F32),
            vmem((S, lang, cols), BF16),
            vmem((N, rows, cols), BF16),
            vmem((Y, 2, share, depth), F32),
            vmem((N, Y, share, depth), F32),
            vmem((N, Y, share, depth), BF16),
            vmem((N, Y, share, depth), BF16),
            vmem((N, Y - 1, share, depth), BF16),
            vmem((N, Y - 1, share, depth), BF16),
            vmem((N, share, depth), BF16),
            vmem((N, share, depth), BF16),
            sem((N,)),
            sem((T, N)),
            sem((2 * Y - 1, N)),
            sem((N,)),
            sem((S - 1, G)),
            sem((G,)),
            sem((G - 1,)),
            sem((S,)),
            sem((S,)),
            sem((S,)),
            sem((S,)),
            sem((T,)),
            sem((T,)),
            sem((S,)),
            sem((S,)),
            sem((G,)),
            sem((S, G)),
            sem((N,)),
            sem((N,)),
            sem((N,)),
            sem((N, Y - 1)),
            sem((N, Y - 1)),
            sem((N,)),
            sem((N,)),
            sem,
        ],
        compiler_params=pltpu.CompilerParams(
            collective_id=0, has_side_effects=True, vmem_limit_bytes=58 * 1024 * 1024
        ),
        cost_estimate=pl.CostEstimate(
            flops=4 * N * rows * depth * cols, bytes_accessed=16 * 1024 * 1024, transcendentals=0
        ),
    )(
        vision,
        vision_gain[None, :],
        vision_bias[None, :],
        weight,
        text,
        gain[None, :],
        slots[None, :],
        cotangent,
    )


def vision_backward(gathered, vision_gain, own_hat, own_inv):
    normed_grad = gathered.transpose(1, 0, 2).reshape(own_hat.shape).astype(jnp.float32)
    weighted = normed_grad * vision_gain
    weighted_mean = jnp.mean(weighted, axis=1, keepdims=True)
    vision_cross = jnp.mean(weighted * own_hat, axis=1, keepdims=True)
    vision_grad = own_inv * (weighted - weighted_mean - own_hat * vision_cross)
    return vision_grad.astype(jnp.bfloat16)


def shards(
    vision_rows,
    vision_gain,
    vision_bias,
    proj_weight,
    text_rows,
    text_gain,
    slot_of_row,
    out_cotangent,
):
    sections = lax.axis_size("section")
    groups = lax.axis_size("dp")
    tensor_count = lax.axis_size("tensor")
    row_total = vision_rows.shape[0]
    lang_total = text_rows.shape[0]
    column_count = text_rows.shape[1]
    unit_total = row_total // UNIT
    lang_units = lang_total // UNIT
    capacity = unit_total // sections
    bucket_count = sections * capacity
    column_total = vision_rows.shape[1]
    depth = proj_weight.shape[0]
    parts = sections * groups
    if (
        min(sections, groups) > 1
        and parts <= 8
        and tensor_count == 4
        and row_total == 128
        and lang_total == 128
        and column_total % 128 == 0
    ):
        return exchange(
            sections,
            groups,
            tensor_count,
            vision_rows,
            vision_gain,
            vision_bias,
            proj_weight,
            text_rows,
            text_gain,
            slot_of_row,
            out_cotangent,
        )
    share = row_total // tensor_count
    share_start = lax.axis_index("tensor") * share
    own_rows = lax.dynamic_slice_in_dim(vision_rows, share_start, share, 0)
    vision_wide = own_rows.astype(jnp.float32)
    centered = vision_wide - jnp.mean(vision_wide, axis=1, keepdims=True)
    own_inv = lax.rsqrt(jnp.mean(centered * centered, axis=1, keepdims=True) + VISION_EPS)
    own_hat = centered * own_inv
    normed_vision = (own_hat * vision_gain + vision_bias).astype(jnp.bfloat16)
    outgoing = normed_vision.reshape(share, parts, depth).transpose(1, 0, 2)
    incoming = lax.all_to_all(
        outgoing, ("section", "dp"), split_axis=0, concat_axis=0, tiled=True
    )
    rows_all = lax.all_gather(incoming, "tensor", axis=1, tiled=True)
    rows_all = rows_all.reshape(parts * row_total, depth)
    partial_out = jnp.dot(rows_all, proj_weight, preferred_element_type=jnp.float32)
    projected = lax.psum_scatter(
        partial_out.astype(jnp.bfloat16), ("section", "dp"), scatter_dimension=0, tiled=True
    ).astype(jnp.float32)
    features = gelu_value(projected).astype(jnp.bfloat16)
    unit_slot = slot_of_row.reshape(unit_total, UNIT)[:, 0]
    unit_live = unit_slot >= 0
    target_device = jnp.where(unit_live, unit_slot // lang_total, 0) // groups
    same_target = (
        (target_device[:, None] == target_device[None, :]) & unit_live[:, None] & unit_live[None, :]
    )
    unit_order = jnp.arange(unit_total)
    earlier = unit_order[None, :] < unit_order[:, None]
    unit_rank = jnp.sum((same_target & earlier).astype(jnp.int32), axis=1)
    bucket = jnp.clip(target_device * capacity + unit_rank, 0, bucket_count - 1)
    chosen = (jnp.arange(bucket_count)[:, None] == bucket[None, :]) & unit_live[None, :]
    chosen_int = chosen.astype(jnp.int32)
    bucket_used = jnp.sum(chosen_int, axis=1) > 0
    bucket_source = jnp.sum(chosen_int * unit_order[None, :], axis=1)
    feature_units = features.reshape(unit_total, UNIT * column_count)
    send_rows = jnp.where(
        bucket_used[:, None], feature_units[bucket_source], jnp.zeros((), jnp.bfloat16)
    )
    send_slots = jnp.where(bucket_used, jnp.sum(chosen_int * unit_slot[None, :], axis=1), -1)
    arrived, arrived_slots = (
        lax.all_to_all(
            send_rows.reshape(sections, capacity * UNIT, column_count),
            "section",
            split_axis=0,
            concat_axis=0,
            tiled=True,
        ),
        lax.all_to_all(
            send_slots.reshape(sections, capacity),
            "section",
            split_axis=0,
            concat_axis=0,
            tiled=True,
        ),
    )
    lang_index = lax.axis_index("section") * groups + lax.axis_index("dp")
    arrived_slots = arrived_slots.reshape(bucket_count)
    arrived_live = arrived_slots >= 0
    arrived_position = jnp.clip(
        (arrived_slots - lang_index * lang_total) // UNIT, 0, lang_units - 1
    )
    placement = (jnp.arange(lang_units)[:, None] == arrived_position[None, :]) & arrived_live[
        None, :
    ]
    placement_int = placement.astype(jnp.int32)
    slot_is_image = jnp.sum(placement_int, axis=1) > 0
    slot_source = jnp.sum(placement_int * jnp.arange(bucket_count)[None, :], axis=1)
    arrived_units = arrived.reshape(bucket_count, UNIT * column_count)
    hidden_units = jnp.where(
        slot_is_image[:, None],
        arrived_units[slot_source],
        text_rows.reshape(lang_units, UNIT * column_count),
    )
    hidden_wide = hidden_units.reshape(lang_total, column_count).astype(jnp.float32)
    upstream = out_cotangent.astype(jnp.float32) * text_gain
    sums = jnp.stack(
        [jnp.sum(hidden_wide * hidden_wide, axis=1), jnp.sum(upstream * hidden_wide, axis=1)]
    )
    square_total, cross_total = lax.psum(sums, "tensor")
    hidden_inv = lax.rsqrt(square_total / D + EPSILON)[:, None]
    normed = (hidden_wide * hidden_inv * text_gain).astype(jnp.bfloat16)
    cross_mean = (cross_total / D)[:, None]
    hidden_grad = (
        hidden_inv * (upstream - hidden_wide * hidden_inv * hidden_inv * cross_mean)
    ).astype(jnp.bfloat16)
    grad_units = hidden_grad.reshape(lang_units, UNIT * column_count)
    reply_rows = jnp.where(
        arrived_live[:, None], grad_units[arrived_position], jnp.zeros((), jnp.bfloat16)
    )
    returned = lax.all_to_all(
        reply_rows.reshape(sections, capacity * UNIT, column_count),
        "section",
        split_axis=0,
        concat_axis=0,
        tiled=True,
    )
    returned_units = returned.reshape(bucket_count, UNIT * column_count)
    feature_grad = jnp.where(
        unit_live[:, None], returned_units[bucket], jnp.zeros((), jnp.bfloat16)
    )
    feature_grad = feature_grad.reshape(row_total, column_count)
    projected_grad = (feature_grad.astype(jnp.float32) * gelu_slope(projected)).astype(jnp.bfloat16)
    grad_all = lax.all_gather(projected_grad, ("section", "dp"), axis=0, tiled=True)
    contract_dims = (((1,), (1,)), ((), ()))
    partial_grad = lax.dot_general(
        grad_all, proj_weight, contract_dims, preferred_element_type=jnp.float32
    )
    partial_grad = partial_grad.astype(jnp.bfloat16).reshape(parts, row_total, depth)
    summed = lax.psum_scatter(partial_grad, "tensor", scatter_dimension=1, tiled=True)
    gathered = lax.all_to_all(
        summed, ("section", "dp"), split_axis=0, concat_axis=0, tiled=True
    )
    return normed, vision_backward(gathered, vision_gain, own_hat, own_inv)


def solution(mesh):
    in_specs = (
        P(("section", "dp"), None),
        P(),
        P(),
        P(("section", "dp"), "tensor"),
        P(("section", "dp"), "tensor"),
        P("tensor"),
        P(("section", "dp")),
        P(("section", "dp"), "tensor"),
    )
    out_specs = (P(("section", "dp"), "tensor"), P(("section", "dp", "tensor"), None))
    return jax.shard_map(shards, mesh=mesh, in_specs=in_specs, out_specs=out_specs, check_vma=False)
```

```python
import functools

import jax
import jax.numpy as jnp
from jax import lax
from jax.experimental import pallas as pl
from jax.experimental.pallas import tpu as pltpu
from jax.sharding import PartitionSpec as P

D = 4096
UNIT = 16


VISION_EPS = 1e-05
EPSILON = 1e-06
HALF_ROOT = 0.7071067811865476
INV_ROOT_TWO_PI = 0.3989422804014327


def gelu_value(values):
    return 0.5 * values * (1.0 + lax.erf(values * HALF_ROOT))


def gelu_slope(values):
    return (
        0.5 * (1.0 + lax.erf(values * HALF_ROOT))
        + values * jnp.exp(-0.5 * values * values) * INV_ROOT_TWO_PI
    )


MESH = pl.DeviceIdType.MESH
BF16 = jnp.bfloat16
F32 = jnp.float32
WAVES = 2


def exchange_kernel(
    sections,
    groups,
    tensor_count,
    vision,
    vision_gain,
    vision_bias,
    weight,
    text,
    gain,
    slots,
    cotangent,
    normed_out,
    grad_out,
    raw,
    x_in,
    hat,
    inverse,
    slots_row,
    x_all,
    product,
    own,
    part_send,
    part_recv,
    group_send,
    group_recv,
    slope,
    features,
    slots_all,
    hidden_all,
    stats,
    reply_send,
    reply_recv,
    pg_all,
    grad_part,
    keep,
    core_send,
    core_recv,
    y_send,
    y_recv,
    last_send,
    last_recv,
    x_ssem,
    x_rsem,
    fwd_ssem,
    part_ssem,
    part_rsem,
    group_ssem,
    group_rsem,
    feat_ssem,
    feat_rsem,
    slot_ssem,
    slot_rsem,
    stat_ssem,
    stat_rsem,
    reply_ssem,
    reply_rsem,
    pgz_ssem,
    pgx_ssem,
    pg_rsem,
    core_ssem,
    core_rsem,
    y_ssem,
    y_rsem,
    last_ssem,
    last_rsem,
    raw_sem,
):
    S, G, T, W = sections, groups, tensor_count, WAVES
    N, Y = S * G, T // 2
    s = lax.axis_index("section")
    d = lax.axis_index("dp")
    t = lax.axis_index("tensor")
    y, c = t // 2, t % 2
    me = s * G + d
    mate = y * 2 + 1 - c
    depth, cols = weight.shape
    column_total = vision.shape[1]
    share = raw.shape[0]
    piece = share // W
    rows = piece * T
    lang = text.shape[0]

    def send(src, dst, ssem, rsem, device):
        pltpu.make_async_remote_copy(
            src_ref=src,
            dst_ref=dst,
            send_sem=ssem,
            recv_sem=rsem,
            device_id=device,
            device_id_type=MESH,
        ).start()

    def arrived(ref, sem):
        pltpu.make_async_copy(ref, ref, sem).wait()

    def loop(first, last, body):
        def step(i, carry):
            body(i)
            return carry

        lax.fori_loop(first, last, step, 0)

    def stage(q, body):
        @pl.when((q >= 0) & (q < W * G))
        def _():
            body(q // G, q % G)

    barrier = pltpu.get_barrier_semaphore()

    def greet(i):
        @pl.when(i != me)
        def _():
            pl.semaphore_signal(barrier, inc=1, device_id=(i // G, i % G, t), device_id_type=MESH)

    fetch = pltpu.make_async_copy(vision.at[pl.ds(t * share, share)], raw, raw_sem)
    fetch.start()
    loop(0, N, greet)
    for dt in range(1, T):
        pl.semaphore_signal(barrier, inc=1, device_id=(s, d, (t + dt) % T), device_id_type=MESH)
    fetch.wait()
    sums = jnp.zeros((share, 128), F32)
    for at in range(0, column_total, 128):
        sums = sums + raw[:, at : at + 128].astype(F32)
    mean = jnp.sum(sums, axis=1, keepdims=True) / column_total
    sums = jnp.zeros((share, 128), F32)
    for at in range(0, column_total, 128):
        centered = raw[:, at : at + 128].astype(F32) - mean
        sums = sums + centered * centered
    square_mean = jnp.sum(sums, axis=1, keepdims=True) / column_total
    inverse[...] = jnp.broadcast_to(lax.rsqrt(square_mean + VISION_EPS), (share, 128))
    own_inv = inverse[:, 0:1]
    for n in range(N):
        span = slice(n * depth, (n + 1) * depth)
        own_hat = (raw[:, span].astype(F32) - mean) * own_inv
        hat[n] = own_hat
        x_in[n] = (
            (own_hat * vision_gain[:, span] + vision_bias[:, span])
            .astype(BF16)
            .reshape(W, piece, depth)
        )
    slots_row[...] = jnp.full(slots_row.shape, -1, jnp.int32)
    slots_row[0:W] = slots[...]
    slots_all[0] = slots_row[...]
    pl.semaphore_wait(barrier, N - 1 + T - 1)

    def send_x(i):
        w, j = i // N, i % N
        to_s, to_d = (s + j % S + 1) % S, (d + j // S + 1) % G
        n = to_s * G + to_d
        k = w * N + d * S + s

        @pl.when(n != me)
        def _():
            send(
                x_in.at[n, w],
                x_all.at[k, t],
                x_ssem.at[w * N + n],
                x_rsem.at[k, t],
                (to_s, to_d, t),
            )

    loop(0, W * N, send_x)
    for w in range(W):
        x_all[w * N + d * S + s, t] = x_in[me, w]
    for js in range(1, S):
        peer = ((s + js) % S, d, t)
        send(slots_row, slots_all.at[S - js], slot_ssem.at[js], slot_rsem.at[S - js], peer)

    def forward_group(w, j):
        at_d = (d - j - 1 + G) % G

        def forward_block(i):
            at_s = (s - i - 1 + S) % S
            k = (w * G + at_d) * S + at_s
            block = x_all.at[k, t]

            @pl.when((at_d != d) | (at_s != s))
            def _():
                arrived(block, x_rsem.at[k, t])

            for dy in range(1, Y):
                peer = ((y + dy) % Y) * 2 + c
                send(block, block, fwd_ssem.at[dy, k], x_rsem.at[k, t], (s, d, peer))
            send(block, block, fwd_ssem.at[0, k], x_rsem.at[k, t], (s, d, mate))

        loop(0, S, forward_block)

    def mate_group(w, j):
        at_d = (d - j - 1 + G) % G

        def mate_block(i):
            k = (w * G + at_d) * S + i
            for dy in range(1, Y):
                other = ((y + dy) % Y) * 2 + c
                block = x_all.at[k, other]
                arrived(block, x_rsem.at[k, other])
                send(block, block, fwd_ssem.at[Y - 1 + dy, k], x_rsem.at[k, other], (s, d, mate))

        loop(0, S, mate_block)

    def project_group(w, j):
        at_d = (d - j - 1 + G) % G
        at = w * G + at_d

        def mate_arrived(i):
            for at_y in range(Y):
                other = at_y * 2 + 1 - c
                arrived(x_all.at[at * S + i, other], x_rsem.at[at * S + i, other])

        loop(0, S, mate_arrived)
        block = x_all[pl.ds(at * S, S)].reshape(S * rows, depth)
        product[...] = jnp.dot(block, weight[...], preferred_element_type=F32).reshape(
            S, rows, cols
        )
        own[at] = product[s]
        for js in range(1, S):
            at_s = (s + js) % S
            part_send[at, js - 1] = product[at_s].astype(BF16)
            send(
                part_send.at[at, js - 1],
                part_recv.at[S - js - 1, at],
                part_ssem.at[js - 1, at],
                part_rsem.at[S - js - 1, at],
                (at_s, d, t),
            )

    def combine_group(w, j):
        at_d = (d - j - 1 + G) % G
        at = w * G + at_d
        total = own[at]
        for js in range(1, S):
            arrived(part_recv.at[js - 1, at], part_rsem.at[js - 1, at])
            total = total + part_recv[js - 1, at].astype(F32)

        own[at] = total

        @pl.when(at_d != d)
        def _():
            group_send[at] = total.astype(BF16)
            slot = (d - at_d + G) % G - 1
            send(
                group_send.at[at],
                group_recv.at[w, slot],
                group_ssem.at[at],
                group_rsem.at[w, slot],
                (s, at_d, t),
            )

    def forward_tick(q):
        stage(q, forward_group)
        stage(q - 1, mate_group)
        stage(q - 2, project_group)
        stage(q - 3, combine_group)

    def finish_projection(w):
        projected = own[w * G + d]
        for slot in range(G - 1):
            arrived(group_recv.at[w, slot], group_rsem.at[w, slot])
            projected = projected + group_recv[w, slot].astype(F32)
        features[w, 0] = gelu_value(projected).astype(BF16)
        for js in range(1, S):
            peer = ((s + js) % S, d, t)
            send(
                features.at[w, 0],
                features.at[w, S - js],
                feat_ssem.at[w, js],
                feat_rsem.at[w, S - js],
                peer,
            )
        slope[w] = gelu_slope(projected)

    def placement(w):
        slot_ids = me * lang + lax.broadcasted_iota(jnp.int32, (lang, rows), 0)
        placed = jnp.zeros((lang, cols), F32)
        taken = jnp.zeros((lang, 1), F32)
        for js in range(S):
            if js > 0:
                arrived(features.at[w, js], feat_rsem.at[w, js])
            chosen = jnp.where(slots_all[js, w : w + 1, :] == slot_ids, 1.0, 0.0)
            taken = taken + jnp.sum(chosen, axis=1, keepdims=True)
            placed = placed + jnp.dot(
                chosen.astype(BF16), features[w, js], preferred_element_type=F32
            )
        hidden = jnp.where(taken > 0.5, placed, text[...].astype(F32))
        hidden_all[w] = hidden
        upstream = cotangent[...].astype(F32) * gain[...]
        squares = jnp.sum(hidden * hidden, axis=1, keepdims=True)
        crosses = jnp.sum(upstream * hidden, axis=1, keepdims=True)
        lanes = lax.broadcasted_iota(jnp.int32, (lang, 128), 1)
        stats[w, 0] = jnp.where(lanes % 8 < 4, squares, crosses).T[0:8]
        for dt in range(1, T):
            send(
                stats.at[w, 0],
                stats.at[w, T - dt],
                stat_ssem.at[w, dt],
                stat_rsem.at[w, T - dt],
                (s, d, (t + dt) % T),
            )
        return taken

    def reply(w, taken):
        total = stats[w, 0]
        for dt in range(1, T):
            arrived(stats.at[w, dt], stat_rsem.at[w, dt])
            total = total + stats[w, dt]
        total = jnp.concatenate([total] * (128 // 8), axis=0).T
        hidden_inv = lax.rsqrt(total[:, 0:1] / D + EPSILON)
        cross_mean = total[:, 4:5] / D
        hidden = hidden_all[w]
        upstream = cotangent[...].astype(F32) * gain[...]
        grads = (
            hidden_inv * (upstream - hidden * hidden_inv * hidden_inv * cross_mean)
        ).astype(BF16)
        lane_ids = me * lang + lax.broadcasted_iota(jnp.int32, (rows, lang), 1)
        for js in reversed(range(S)):
            named = slots_all[js, w : w + 1, :]
            named = jnp.concatenate([named] * (128 // rows), axis=1)
            named = jnp.broadcast_to(named, (128, 128)).T[0:rows]
            chosen = jnp.where(named == lane_ids, 1.0, 0.0).astype(BF16)
            answer = jnp.dot(chosen, grads, preferred_element_type=F32).astype(BF16)
            if js == 0:
                reply_recv[w, 0] = answer
            else:
                reply_send[w, js] = answer
                send(
                    reply_send.at[w, js],
                    reply_recv.at[w, S - js],
                    reply_ssem.at[w, js],
                    reply_rsem.at[w, S - js],
                    ((s + js) % S, d, t),
                )
        normed = (hidden * hidden_inv * gain[...]).astype(BF16)
        if w > 0:
            normed = jnp.where(taken > 0.5, normed.astype(F32), normed_out[...].astype(F32))
        normed_out[...] = normed.astype(BF16)

    def start_back(w):
        feature_grad = reply_recv[w, 0].astype(F32)
        for js in range(1, S):
            arrived(reply_recv.at[w, js], reply_rsem.at[w, js])
            feature_grad = feature_grad + reply_recv[w, js].astype(F32)
        k = (w * G + d) * S + s
        pg_all[k] = (feature_grad * slope[w]).astype(BF16)
        for jd in range(1, G):
            send(
                pg_all.at[k],
                pg_all.at[k],
                pgz_ssem.at[w, jd],
                pg_rsem.at[k],
                (s, (d + jd) % G, t),
            )

    def spread_group(w, j):
        at_d = (d - j + G) % G
        at = w * G + at_d
        k = at * S + s

        @pl.when(j > 0)
        def _():
            arrived(pg_all.at[k], pg_rsem.at[k])

        for js in range(1, S):
            send(
                pg_all.at[k],
                pg_all.at[k],
                pgx_ssem.at[js, at],
                pg_rsem.at[k],
                ((s + js) % S, d, t),
            )

    def back_group(w, j):
        at = w * G + (d - j + G) % G
        for js in range(1, S):
            k = at * S + (s + js) % S
            arrived(pg_all.at[k], pg_rsem.at[k])
        grad_part[...] = lax.dot_general(
            pg_all[pl.ds(at * S, S)].reshape(S * rows, cols),
            weight[...],
            (((1,), (1,)), ((), ())),
            preferred_element_type=F32,
        ).reshape(S, Y, 2, piece, depth)
        for at_y in range(Y):
            keep[at, at_y] = grad_part[:, at_y, c]
            core_send[at, at_y] = grad_part[:, at_y, 1 - c].astype(BF16)
        send(core_send.at[at], core_recv.at[at], core_ssem.at[at], core_rsem.at[at], (s, d, mate))

    def reduce_cores(w, j):
        at = w * G + (d - j + G) % G
        arrived(core_recv.at[at], core_rsem.at[at])
        for dy in range(1, Y):
            to_y = (y + dy) % Y
            y_send[at, dy - 1] = (keep[at, to_y] + core_recv[at, to_y].astype(F32)).astype(BF16)
            send(
                y_send.at[at, dy - 1],
                y_recv.at[at, Y - dy - 1],
                y_ssem.at[at, dy - 1],
                y_rsem.at[at, Y - dy - 1],
                (s, d, to_y * 2 + c),
            )
        keep[at, y] = keep[at, y] + core_recv[at, y].astype(F32)

    def finish_group(w, j):
        at_d = (d - j + G) % G
        at = w * G + at_d
        total = keep[at, y]
        for dy in range(1, Y):
            arrived(y_recv.at[at, dy - 1], y_rsem.at[at, dy - 1])
            total = total + y_recv[at, dy - 1].astype(F32)
        last_send[at] = total.astype(BF16)
        for js in range(S):
            at_s = (s + js) % S

            def push():
                send(
                    last_send.at[at, at_s],
                    last_recv.at[me, w],
                    last_ssem.at[at, at_s],
                    last_rsem.at[me, w],
                    (at_s, at_d, t),
                )

            if js > 0:
                push()
            else:
                pl.when(j > 0)(push)

    def back_tick(q):
        stage(q, spread_group)
        stage(q - 1, back_group)
        stage(q - 2, reduce_cores)
        stage(q - 3, finish_group)

    loop(0, G + 3, forward_tick)
    for js in range(1, S):
        arrived(slots_all.at[js], slot_rsem.at[js])
    finish_projection(0)
    loop(G + 3, W * G + 3, forward_tick)
    taken_first = placement(0)
    finish_projection(1)
    reply(0, taken_first)
    taken_later = placement(1)
    start_back(0)
    reply(1, taken_later)
    loop(0, 2, back_tick)
    start_back(1)
    loop(2, W * G + 3, back_tick)

    for w in range(W):
        last_recv[me, w] = last_send[w * G + d, s]

    def collect(n):
        @pl.when(n != me)
        def _():
            for w in range(W):
                arrived(last_recv.at[n, w], last_rsem.at[n, w])

    loop(0, N, collect)
    plain = jnp.zeros((share, 1), F32)
    crossed = jnp.zeros((share, 1), F32)
    for n in range(N):
        span = slice(n * depth, (n + 1) * depth)
        weighted = last_recv[n].reshape(share, depth).astype(F32) * vision_gain[:, span]
        plain = plain + jnp.sum(weighted, axis=1, keepdims=True)
        crossed = crossed + jnp.sum(weighted * hat[n], axis=1, keepdims=True)
    plain = plain / column_total
    crossed = crossed / column_total
    own_inv = inverse[:, 0:1]
    for n in range(N):
        span = slice(n * depth, (n + 1) * depth)
        weighted = last_recv[n].reshape(share, depth).astype(F32) * vision_gain[:, span]
        grad_out[:, span] = (own_inv * (weighted - plain - hat[n] * crossed)).astype(BF16)

    def drain_block(k):
        w, n = k // N, k % N

        @pl.when(n != me)
        def _():
            arrived(x_in.at[n, w], x_ssem.at[k])

        for i in range(2 * Y - 1):
            arrived(x_all.at[k, t], fwd_ssem.at[i, k])

    loop(0, W * N, drain_block)

    def drain_group(at):
        for js in range(1, S):
            arrived(part_send.at[at, js - 1], part_ssem.at[js - 1, at])
            arrived(pg_all.at[0], pgx_ssem.at[js, at])
        arrived(core_send.at[at], core_ssem.at[at])
        for dy in range(1, Y):
            arrived(y_send.at[at, dy - 1], y_ssem.at[at, dy - 1])

        @pl.when(at % G != d)
        def _():
            arrived(group_send.at[at], group_ssem.at[at])

        for at_s in range(S):

            @pl.when((at % G != d) | (s != at_s))
            def _():
                arrived(last_send.at[at, at_s], last_ssem.at[at, at_s])

    loop(0, W * G, drain_group)
    for js in range(1, S):
        arrived(slots_row, slot_ssem.at[js])
    for w in range(W):
        for jd in range(1, G):
            arrived(pg_all.at[0], pgz_ssem.at[w, jd])
        for js in range(1, S):
            arrived(features.at[w, 0], feat_ssem.at[w, js])
            arrived(reply_send.at[w, js], reply_ssem.at[w, js])
        for dt in range(1, T):
            arrived(stats.at[w, 0], stat_ssem.at[w, dt])


def exchange(
    S, G, T, vision, vision_gain, vision_bias, weight, text, gain, slots, cotangent
):
    N, Y = S * G, T // 2
    rows, column_total = vision.shape
    share, depth = rows // T, weight.shape[0]
    lang, cols = text.shape
    W = WAVES
    piece = share // W
    part = piece * T
    sem = pltpu.SemaphoreType.DMA
    vmem = pltpu.VMEM
    whole = pl.BlockSpec(memory_space=pltpu.VMEM)
    return pl.pallas_call(
        functools.partial(exchange_kernel, S, G, T),
        out_shape=(
            jax.ShapeDtypeStruct((lang, cols), BF16),
            jax.ShapeDtypeStruct((share, column_total), BF16),
        ),
        in_specs=[pl.BlockSpec(memory_space=pl.ANY)] + [whole] * 7,
        out_specs=(whole, whole),
        scratch_shapes=[
            vmem((share, column_total), BF16),
            vmem((N, W, piece, depth), BF16),
            vmem((N, share, depth), F32),
            vmem((share, 128), F32),
            vmem((8, part), jnp.int32),
            vmem((W * N, T, piece, depth), BF16),
            vmem((S, part, cols), F32),
            vmem((W * G, part, cols), F32),
            vmem((W * G, S - 1, part, cols), BF16),
            vmem((S - 1, W * G, part, cols), BF16),
            vmem((W * G, part, cols), BF16),
            vmem((W, G - 1, part, cols), BF16),
            vmem((W, part, cols), F32),
            vmem((W, S, part, cols), BF16),
            vmem((S, 8, part), jnp.int32),
            vmem((W, lang, cols), F32),
            vmem((W, T, 8, lang), F32),
            vmem((W, S, part, cols), BF16),
            vmem((W, S, part, cols), BF16),
            vmem((W * N, part, cols), BF16),
            vmem((S, Y, 2, piece, depth), F32),
            vmem((W * G, Y, S, piece, depth), F32),
            vmem((W * G, Y, S, piece, depth), BF16),
            vmem((W * G, Y, S, piece, depth), BF16),
            vmem((W * G, Y - 1, S, piece, depth), BF16),
            vmem((W * G, Y - 1, S, piece, depth), BF16),
            vmem((W * G, S, piece, depth), BF16),
            vmem((N, W, piece, depth), BF16),
            sem((W * N,)),
            sem((W * N, T)),
            sem((2 * Y - 1, W * N)),
            sem((S - 1, W * G)),
            sem((S - 1, W * G)),
            sem((W * G,)),
            sem((W, G - 1)),
            sem((W, S)),
            sem((W, S)),
            sem((S,)),
            sem((S,)),
            sem((W, T)),
            sem((W, T)),
            sem((W, S)),
            sem((W, S)),
            sem((W, G)),
            sem((S, W * G)),
            sem((W * N,)),
            sem((W * G,)),
            sem((W * G,)),
            sem((W * G, Y - 1)),
            sem((W * G, Y - 1)),
            sem((W * G, S)),
            sem((N, W)),
            sem,
        ],
        compiler_params=pltpu.CompilerParams(
            collective_id=0, has_side_effects=True, vmem_limit_bytes=58 * 1024 * 1024
        ),
        cost_estimate=pl.CostEstimate(
            flops=4 * N * rows * depth * cols, bytes_accessed=16 * 1024 * 1024, transcendentals=0
        ),
    )(
        vision,
        vision_gain[None, :],
        vision_bias[None, :],
        weight,
        text,
        gain[None, :],
        slots.reshape(T, W, piece).transpose(1, 0, 2).reshape(W, part),
        cotangent,
    )


def vision_backward(gathered, vision_gain, own_hat, own_inv):
    normed_grad = gathered.transpose(1, 0, 2).reshape(own_hat.shape).astype(jnp.float32)
    weighted = normed_grad * vision_gain
    weighted_mean = jnp.mean(weighted, axis=1, keepdims=True)
    vision_cross = jnp.mean(weighted * own_hat, axis=1, keepdims=True)
    vision_grad = own_inv * (weighted - weighted_mean - own_hat * vision_cross)
    return vision_grad.astype(jnp.bfloat16)


def shards(
    vision_rows,
    vision_gain,
    vision_bias,
    proj_weight,
    text_rows,
    text_gain,
    slot_of_row,
    out_cotangent,
):
    sections = lax.axis_size("section")
    groups = lax.axis_size("dp")
    tensor_count = lax.axis_size("tensor")
    row_total = vision_rows.shape[0]
    lang_total = text_rows.shape[0]
    column_count = text_rows.shape[1]
    unit_total = row_total // UNIT
    lang_units = lang_total // UNIT
    capacity = unit_total // sections
    bucket_count = sections * capacity
    column_total = vision_rows.shape[1]
    depth = proj_weight.shape[0]
    parts = sections * groups
    if (
        min(sections, groups) > 1
        and parts <= 8
        and tensor_count == 4
        and row_total == 128
        and lang_total == 128
        and column_total % 128 == 0
    ):
        return exchange(
            sections,
            groups,
            tensor_count,
            vision_rows,
            vision_gain,
            vision_bias,
            proj_weight,
            text_rows,
            text_gain,
            slot_of_row,
            out_cotangent,
        )
    share = row_total // tensor_count
    share_start = lax.axis_index("tensor") * share
    own_rows = lax.dynamic_slice_in_dim(vision_rows, share_start, share, 0)
    vision_wide = own_rows.astype(jnp.float32)
    centered = vision_wide - jnp.mean(vision_wide, axis=1, keepdims=True)
    own_inv = lax.rsqrt(jnp.mean(centered * centered, axis=1, keepdims=True) + VISION_EPS)
    own_hat = centered * own_inv
    normed_vision = (own_hat * vision_gain + vision_bias).astype(jnp.bfloat16)
    outgoing = normed_vision.reshape(share, parts, depth).transpose(1, 0, 2)
    incoming = lax.all_to_all(
        outgoing, ("section", "dp"), split_axis=0, concat_axis=0, tiled=True
    )
    rows_all = lax.all_gather(incoming, "tensor", axis=1, tiled=True)
    rows_all = rows_all.reshape(parts * row_total, depth)
    partial_out = jnp.dot(rows_all, proj_weight, preferred_element_type=jnp.float32)
    projected = lax.psum_scatter(
        partial_out.astype(jnp.bfloat16), ("section", "dp"), scatter_dimension=0, tiled=True
    ).astype(jnp.float32)
    features = gelu_value(projected).astype(jnp.bfloat16)
    unit_slot = slot_of_row.reshape(unit_total, UNIT)[:, 0]
    unit_live = unit_slot >= 0
    target_device = jnp.where(unit_live, unit_slot // lang_total, 0) // groups
    same_target = (
        (target_device[:, None] == target_device[None, :]) & unit_live[:, None] & unit_live[None, :]
    )
    unit_order = jnp.arange(unit_total)
    earlier = unit_order[None, :] < unit_order[:, None]
    unit_rank = jnp.sum((same_target & earlier).astype(jnp.int32), axis=1)
    bucket = jnp.clip(target_device * capacity + unit_rank, 0, bucket_count - 1)
    chosen = (jnp.arange(bucket_count)[:, None] == bucket[None, :]) & unit_live[None, :]
    chosen_int = chosen.astype(jnp.int32)
    bucket_used = jnp.sum(chosen_int, axis=1) > 0
    bucket_source = jnp.sum(chosen_int * unit_order[None, :], axis=1)
    feature_units = features.reshape(unit_total, UNIT * column_count)
    send_rows = jnp.where(
        bucket_used[:, None], feature_units[bucket_source], jnp.zeros((), jnp.bfloat16)
    )
    send_slots = jnp.where(bucket_used, jnp.sum(chosen_int * unit_slot[None, :], axis=1), -1)
    arrived, arrived_slots = (
        lax.all_to_all(
            send_rows.reshape(sections, capacity * UNIT, column_count),
            "section",
            split_axis=0,
            concat_axis=0,
            tiled=True,
        ),
        lax.all_to_all(
            send_slots.reshape(sections, capacity),
            "section",
            split_axis=0,
            concat_axis=0,
            tiled=True,
        ),
    )
    lang_index = lax.axis_index("section") * groups + lax.axis_index("dp")
    arrived_slots = arrived_slots.reshape(bucket_count)
    arrived_live = arrived_slots >= 0
    arrived_position = jnp.clip(
        (arrived_slots - lang_index * lang_total) // UNIT, 0, lang_units - 1
    )
    placement = (jnp.arange(lang_units)[:, None] == arrived_position[None, :]) & arrived_live[
        None, :
    ]
    placement_int = placement.astype(jnp.int32)
    slot_is_image = jnp.sum(placement_int, axis=1) > 0
    slot_source = jnp.sum(placement_int * jnp.arange(bucket_count)[None, :], axis=1)
    arrived_units = arrived.reshape(bucket_count, UNIT * column_count)
    hidden_units = jnp.where(
        slot_is_image[:, None],
        arrived_units[slot_source],
        text_rows.reshape(lang_units, UNIT * column_count),
    )
    hidden_wide = hidden_units.reshape(lang_total, column_count).astype(jnp.float32)
    upstream = out_cotangent.astype(jnp.float32) * text_gain
    sums = jnp.stack(
        [jnp.sum(hidden_wide * hidden_wide, axis=1), jnp.sum(upstream * hidden_wide, axis=1)]
    )
    square_total, cross_total = lax.psum(sums, "tensor")
    hidden_inv = lax.rsqrt(square_total / D + EPSILON)[:, None]
    normed = (hidden_wide * hidden_inv * text_gain).astype(jnp.bfloat16)
    cross_mean = (cross_total / D)[:, None]
    hidden_grad = (
        hidden_inv * (upstream - hidden_wide * hidden_inv * hidden_inv * cross_mean)
    ).astype(jnp.bfloat16)
    grad_units = hidden_grad.reshape(lang_units, UNIT * column_count)
    reply_rows = jnp.where(
        arrived_live[:, None], grad_units[arrived_position], jnp.zeros((), jnp.bfloat16)
    )
    returned = lax.all_to_all(
        reply_rows.reshape(sections, capacity * UNIT, column_count),
        "section",
        split_axis=0,
        concat_axis=0,
        tiled=True,
    )
    returned_units = returned.reshape(bucket_count, UNIT * column_count)
    feature_grad = jnp.where(
        unit_live[:, None], returned_units[bucket], jnp.zeros((), jnp.bfloat16)
    )
    feature_grad = feature_grad.reshape(row_total, column_count)
    projected_grad = (feature_grad.astype(jnp.float32) * gelu_slope(projected)).astype(jnp.bfloat16)
    grad_all = lax.all_gather(projected_grad, ("section", "dp"), axis=0, tiled=True)
    contract_dims = (((1,), (1,)), ((), ()))
    partial_grad = lax.dot_general(
        grad_all, proj_weight, contract_dims, preferred_element_type=jnp.float32
    )
    partial_grad = partial_grad.astype(jnp.bfloat16).reshape(parts, row_total, depth)
    summed = lax.psum_scatter(partial_grad, "tensor", scatter_dimension=1, tiled=True)
    gathered = lax.all_to_all(
        summed, ("section", "dp"), split_axis=0, concat_axis=0, tiled=True
    )
    return normed, vision_backward(gathered, vision_gain, own_hat, own_inv)


def solution(mesh):
    in_specs = (
        P(("section", "dp"), None),
        P(),
        P(),
        P(("section", "dp"), "tensor"),
        P(("section", "dp"), "tensor"),
        P("tensor"),
        P(("section", "dp")),
        P(("section", "dp"), "tensor"),
    )
    out_specs = (P(("section", "dp"), "tensor"), P(("section", "dp", "tensor"), None))
    return jax.shard_map(shards, mesh=mesh, in_specs=in_specs, out_specs=out_specs, check_vma=False)
```
